32 devices in a mesh: row: 4 (over z), col: 8 (over y, x, core).
Axes of the slice: x: 2, y: 2, z: 4, core: 2. Of those that a mesh axis runs over, the one named last changes fastest.
Arguments:
- densities: bfloat16 [7680, 4500], P('col'), may hold values from -0.75 to 0.75
- coupling_a: float32 [5, 900], replicated, may hold values from -6 to 6
- coupling_b: float32 [5, 900], replicated, may hold values from -6 to 6
- energies: float32 [7680], replicated, may hold values from 2 to 40
- strength: float32 [7680], replicated, may hold values from -6 to 6
- qp_index: int32 [7680, 2], replicated, may hold values from 0 to 1023
- kpi_label: int32 [7680], replicated, may hold values from 0 to 15
- amplitude_u: float32 [1024], replicated, may hold values from 0.1 to 1
- amplitude_v: float32 [1024], replicated, may hold values from 0.1 to 1
- panel_blocks: int32 [2], replicated, may hold values from 0 to 3, as said below
Outputs:
- matrix_a: float32 [2, 960, 7680], P(None, 'row', 'col')
- matrix_b: float32 [2, 960, 7680], P(None, 'row', 'col')
- response: float32 [2, 960], P(None, 'row')
- mirror: float32 [2, 7680], P(None, 'col')
The draws below stay inside these ranges and needn't reach their ends.
Inputs may be any that keep to these rules, and one draw needn't show every extreme that they name: `panel_blocks`: both blocks lie in the lower half of the column blocks, one of them is block 3, and the two may coincide.
All inputs are finite; a program needn't handle non-finite values.
Results may differ from the reference program's by a relative error of at most 0.007.
Values may be sent and summed in bfloat16 or wider, within the bound.
No kernel may reach another device: no remote copies, remote signals or barrier semaphores. Data moves between devices by JAX's collectives and lax.ppermute only.
A program may use at most 64 MiB of HBM per device.

```python
import math
import jax
import jax.numpy as jnp
from jax import lax

POINTS = 900
TYPES = 5
NQP = 1024
NKPI = 16
COLB = 960
NBLK = 8
NPAIRS = 7680


def draw_panel_blocks(key, part):
    first_key = jax.random.fold_in(key, 7001)
    second_key = jax.random.fold_in(key, 7002)
    top_block = NBLK // 2 - 1
    other = jax.random.randint(first_key, (), 0, NBLK // 2, dtype=jnp.int32)
    flipped = jax.random.randint(second_key, (), 0, 2, dtype=jnp.int32)
    top_value = jnp.full((), top_block, dtype=jnp.int32)
    return jnp.where(flipped == 0, jnp.stack([top_value, other]), jnp.stack([other, top_value])).astype(jnp.int32)


def with_ends(drawn, own_key, low, high):
    longest = drawn.shape.index(max(drawn.shape))
    spots = []
    for shift in (0, 1):
        where = [jax.random.randint(jax.random.fold_in(own_key, axis), (), 0, length) for axis, length in enumerate(drawn.shape)]
        where[longest] = (where[longest] + shift) % drawn.shape[longest]
        spots.append(tuple(where))
    return drawn.at[spots[0]].set(low).at[spots[1]].set(high)


def levels(stream_key, dims, pieces, smallest, high):
    level, own = 1.0, jax.random.fold_in(stream_key, 6)
    for dim, shards_of in pieces:
        steps = jnp.exp(jax.random.uniform(jax.random.fold_in(own, dim), (shards_of,), jnp.float32, smallest / len(pieces), high / len(pieces)))
        level = level * jnp.repeat(steps, dims[dim] // shards_of).reshape([-1 if axis == dim else 1 for axis in range(len(dims))])
    return level


def noise(key, extent, scale, most, split=(), kind=jnp.bfloat16):
    result = scale * jax.random.normal(key, extent, jnp.float32)
    if split:
        result = result * levels(key, extent, split, -0.22, 0.18)
    return jnp.clip(result, -most, most).astype(kind)


def setup_inputs(seed: int = 0) -> dict:
    arg_keys = jax.random.split(jax.random.key(seed), 11)
    return {
        "densities": noise(arg_keys[0], (NPAIRS, TYPES * POINTS), 0.12, 0.75, ((0, 8),)),
        "coupling_a": noise(arg_keys[1], (TYPES, POINTS), 1.0, 6.0, (), jnp.float32),
        "coupling_b": noise(arg_keys[2], (TYPES, POINTS), 1.0, 6.0, (), jnp.float32),
        "energies": jnp.clip(jnp.exp(jax.random.uniform(arg_keys[3], (NPAIRS,), jnp.float32, math.log(2.0), math.log(40.0))), 2.0, 40.0),
        "strength": noise(arg_keys[4], (NPAIRS,), 1.0, 6.0, (), jnp.float32),
        "qp_index": with_ends(jax.random.randint(arg_keys[5], (NPAIRS, 2), 0, NQP), jax.random.fold_in(arg_keys[5], 1), 0, NQP - 1).astype(jnp.int32),
        "kpi_label": with_ends(jax.random.randint(arg_keys[6], (NPAIRS,), 0, NKPI), jax.random.fold_in(arg_keys[6], 1), 0, NKPI - 1).astype(jnp.int32),
        "amplitude_u": jnp.clip(jax.random.uniform(arg_keys[7], (NQP,), jnp.float32, 0.1, 1.0), 0.1, 1.0),
        "amplitude_v": jnp.clip(jax.random.uniform(arg_keys[8], (NQP,), jnp.float32, 0.1, 1.0), 0.1, 1.0),
        "panel_blocks": draw_panel_blocks(jax.random.fold_in(arg_keys[10], 71), 0),
    }


PAIRING = 1.0
HIGH = lax.Precision.HIGHEST

def pair_factors(qp_part, label_part, amplitude_u, amplitude_v):
    states = lax.broadcasted_iota(jnp.int32, (1, amplitude_u.shape[0]), 1)
    amp_table = jnp.stack([amplitude_u, amplitude_v], axis=1)
    first_amp = jnp.dot((qp_part[:, 0:1] == states).astype(jnp.float32), amp_table, precision=HIGH)
    second_amp = jnp.dot((qp_part[:, 1:2] == states).astype(jnp.float32), amp_table, precision=HIGH)
    anomal = first_amp[:, 0] * second_amp[:, 1] + first_amp[:, 1] * second_amp[:, 0]
    direct = first_amp[:, 0] * second_amp[:, 0] - first_amp[:, 1] * second_amp[:, 1]
    labels = lax.broadcasted_iota(jnp.int32, (1, NKPI), 1)
    member = (label_part[:, None] == labels).astype(jnp.float32)
    return (anomal, direct, member)

def reference(densities, coupling_a, coupling_b, energies, strength, qp_index, kpi_label, amplitude_u, amplitude_v, panel_blocks):
    total_pairs = densities.shape[0]
    weight_a = coupling_a.reshape(-1)
    weight_b = coupling_b.reshape(-1)
    anomal, direct, member = pair_factors(qp_index, kpi_label, amplitude_u, amplitude_v)
    col_global = jnp.arange(total_pairs, dtype=jnp.int32)
    col_block = col_global // COLB
    list_a, list_b, list_resp, list_mirror = ([], [], [], [])
    for which in range(2):
        block_id = panel_blocks[which].astype(jnp.int32)
        start = (block_id * COLB).astype(jnp.int32)
        panel = lax.dynamic_slice_in_dim(densities, start, COLB, 0)
        weighted = jnp.concatenate([(panel.astype(jnp.float32) * weight_a).astype(jnp.bfloat16), (panel.astype(jnp.float32) * weight_b).astype(jnp.bfloat16)], 0)
        product = lax.dot_general(weighted, densities, (((1,), (1,)), ((), ())), preferred_element_type=jnp.float32)
        row_anomal = lax.dynamic_slice_in_dim(anomal, start, COLB, 0)
        row_direct = lax.dynamic_slice_in_dim(direct, start, COLB, 0)
        row_member = lax.dynamic_slice_in_dim(member, start, COLB, 0)
        row_energy = lax.dynamic_slice_in_dim(energies, start, COLB, 0)
        row_strength = lax.dynamic_slice_in_dim(strength, start, COLB, 0)
        pair_a = jnp.dot(row_anomal[:, None] * row_member, (anomal[:, None] * member).T, precision=HIGH)
        pair_b = jnp.dot(row_direct[:, None] * row_member, (direct[:, None] * member).T, precision=HIGH)
        row_global = start + jnp.arange(COLB, dtype=jnp.int32)
        diagonal = jnp.where(row_global[:, None] == col_global[None, :], row_energy[:, None], 0.0)
        active = (col_block >= block_id)[None, :]
        mat_a = jnp.where(active, product[:COLB] + diagonal + PAIRING * pair_a, 0.0)
        mat_b = jnp.where(active, product[COLB:] + PAIRING * pair_b, 0.0)
        summed = mat_a + mat_b
        list_resp.append(jnp.dot(summed, strength, precision=HIGH) / math.sqrt(total_pairs))
        list_mirror.append(jnp.dot(row_strength, summed, precision=HIGH) / math.sqrt(COLB))
        list_a.append(mat_a)
        list_b.append(mat_b)
    return (jnp.stack(list_a), jnp.stack(list_b), jnp.stack(list_resp), jnp.stack(list_mirror))
```

```python
import functools
import math

import jax
import jax.numpy as jnp
from jax import lax
from jax.experimental import pallas as pl
from jax.experimental.pallas import tpu as pltpu
from jax.sharding import PartitionSpec as P

NKPI = 16
PAIRING = 1.0
HIGH = lax.Precision.HIGHEST
LANES = 128
PIECES = 4
BRANCHES = 4
VMEM_BYTES = 40 << 20
IN_VMEM = pl.BlockSpec(memory_space=pltpu.VMEM)
IN_SMEM = pl.BlockSpec(memory_space=pltpu.SMEM)
ANYWHERE = pl.BlockSpec(memory_space=pl.ANY)

OWN, R1, R2, R3, R4 = 1, 2, 3, 4, 5
SRC_O, SRC_TOP, LATE, ACT_O, ACT_TOP, PANEL_O, PANEL_TOP, START_O, START_TOP, COL_START = (
    0, 2, 4, 5, 6, 7, 8, 9, 10, 11,
)


def piece_spans(depth):
    tiles = -(-depth // LANES)
    width = LANES * -(-tiles // PIECES)
    return [(lo, min(depth, lo + width)) for lo in range(0, depth, width)], width


def factors(qp_part, amplitude_u, amplitude_v):
    states = lax.broadcasted_iota(jnp.int32, (1, amplitude_u.shape[0]), 1)
    amp_table = jnp.stack([amplitude_u, amplitude_v], axis=1)
    first_amp = jnp.dot((qp_part[:, 0:1] == states).astype(jnp.float32), amp_table, precision=HIGH)
    second_amp = jnp.dot((qp_part[:, 1:2] == states).astype(jnp.float32), amp_table, precision=HIGH)
    anomal = first_amp[:, 0] * second_amp[:, 1] + first_amp[:, 1] * second_amp[:, 0]
    direct = first_amp[:, 0] * second_amp[:, 0] - first_amp[:, 1] * second_amp[:, 1]
    return anomal, direct


def times(left, right):
    return lax.dot_general(
        left, right, (((1,), (1,)), ((), ())), preferred_element_type=jnp.float32
    )


def fetch(flags, at, sources, buf, sems):
    for slot, entry in ((0, SRC_O + at), (1, SRC_TOP + at)):
        for code, ref in sources:

            @pl.when(flags[entry] == code)
            def _():
                pltpu.make_async_copy(ref, buf.at[slot], sems.at[slot]).start()

    for slot, entry in ((0, SRC_O + at), (1, SRC_TOP + at)):

        @pl.when(flags[entry] > 0)
        def _():
            pltpu.make_async_copy(sources[0][1], buf.at[slot], sems.at[slot]).wait()


def weigh(x, weights, which, lo, hi):
    scale = weights[pl.ds(which, 1), lo:hi]
    return (x.astype(jnp.float32) * scale).astype(jnp.bfloat16)


def piece_kernel(at, lo, hi, first, flags, own, r1, r2, r3, r4, dens, weights, *rest):
    if first:
        acc, buf, sems = rest
    else:
        before, acc, buf, sems = rest
    fetch(flags, at, ((OWN, own), (R1, r1), (R2, r2), (R3, r3), (R4, r4)), buf, sems)

    def step(n, carry):
        slot, which = n // 2, n % 2

        @pl.when(flags[SRC_O + 2 * slot + at] > 0)
        def _():
            product = times(weigh(buf[slot, :, : hi - lo], weights, which, lo, hi), dens[:, lo:hi])
            if first:
                acc[slot, which] = product
            else:
                acc[slot, which] = before[slot, which] + product

        return carry

    lax.fori_loop(0, 4, step, 0)


def late_kernel(spans, width, flags, l0, l1, l2, dens, weights, before, acc, buf, sem):
    for code, ref in ((1, l0), (2, l1), (3, l2)):

        @pl.when(flags[LATE] == code)
        def _():
            pltpu.make_async_copy(ref, buf, sem).start()

    @pl.when(flags[LATE] > 0)
    def _():
        pltpu.make_async_copy(l0, buf, sem).wait()

        def step(which, carry):
            lo, hi = spans[-1]
            acc[0, which] = times(weigh(buf[:, lo:hi], weights, which, lo, hi), dens[:, lo:hi])

            def add(piece, carry):
                span = pl.ds(pl.multiple_of(piece * width, LANES), width)
                x = buf[:, span].astype(jnp.float32) * weights[pl.ds(which, 1), span]
                acc[0, which] += times(x.astype(jnp.bfloat16), dens[:, span])
                return carry

            lax.fori_loop(0, len(spans) - 1, add, 0)
            return carry

        lax.fori_loop(0, 2, step, 0)


def last_kernel(
    at, lo, hi, flags, own, r1, r2, r3, r4, dens, weights, cols, rows, labels, before,
    mat_a, mat_b, resp, mirror, buf, made, sems, out_sems,
):
    fetch(flags, at, ((OWN, own), (R1, r1), (R2, r2), (R3, r3), (R4, r4)), buf, sems)
    resp[...] = jnp.zeros_like(resp)
    mirror[...] = jnp.zeros_like(mirror)
    row_len, block_len = made.shape[2:]
    row_ids = lax.broadcasted_iota(jnp.int32, (row_len, block_len), 0)
    col_ids = lax.broadcasted_iota(jnp.int32, (row_len, block_len), 1) + flags[COL_START]

    def out_copies(slot, panel):
        return [
            pltpu.make_async_copy(made.at[slot, 0], mat_a.at[panel], out_sems.at[slot, 0]),
            pltpu.make_async_copy(made.at[slot, 1], mat_b.at[panel], out_sems.at[slot, 1]),
        ]

    def step(slot, carry):
        panel = flags[PANEL_O + slot]

        @pl.when(flags[ACT_O + slot] > 0)
        def _():
            made[slot] = before[slot]

            @pl.when(flags[SRC_O + 2 * slot + at] > 0)
            def _():
                def add(which, carry):
                    x = weigh(buf[slot, :, : hi - lo], weights, which, lo, hi)
                    made[slot, which] += times(x, dens[:, lo:hi])
                    return carry

                lax.fori_loop(0, 2, add, 0)

            same = labels[slot] == cols[3:4].astype(jnp.int32)
            diagonal = row_ids + flags[START_O + slot] == col_ids
            row = rows[slot]
            full_a = made[slot, 0] + jnp.where(diagonal, row[:, 2:3], 0.0)
            full_a = full_a + jnp.where(same, PAIRING * (row[:, 0:1] * cols[0:1]), 0.0)
            full_b = made[slot, 1] + jnp.where(same, PAIRING * (row[:, 1:2] * cols[1:2]), 0.0)
            made[slot, 0] = full_a
            made[slot, 1] = full_b
            both = full_a + full_b
            across = jnp.sum(both * cols[2:3], axis=1, keepdims=True)
            resp[pl.ds(panel, 1), :] = jnp.broadcast_to(across, (row_len, LANES)).T[0:1]
            mirror[pl.ds(panel, 1), :] = jnp.sum(both * row[:, 3:4], axis=0, keepdims=True)

        @pl.when(flags[ACT_O + slot] == 0)
        def _():
            made[slot] = jnp.zeros_like(made[slot])

        for copy in out_copies(slot, panel):
            copy.start()
        return carry

    lax.fori_loop(0, 2, step, 0)
    for slot in range(2):
        for copy in out_copies(slot, flags[PANEL_O + slot]):
            copy.wait()


def cost(flops, moved):
    return pl.CostEstimate(flops=flops, bytes_accessed=moved, transcendentals=0)


def all_sum(value, axis):
    size = lax.axis_size(axis)
    if size & (size - 1):
        return lax.psum(value, axis)
    step = 1
    while step < size:
        value = value + lax.ppermute(value, axis, [(i, i ^ step) for i in range(size)])
        step *= 2
    return value


def on_device(
    densities,
    coupling_a,
    coupling_b,
    energies,
    strength,
    qp_index,
    kpi_label,
    amplitude_u,
    amplitude_v,
    panel_blocks,
):
    block_len, depth = densities.shape
    row_count = lax.axis_size("row")
    cols = lax.axis_size("col")
    half = cols // 2
    top = half - 1
    row_len = block_len // row_count
    row_pos = lax.axis_index("row")
    col_pos = lax.axis_index("col")
    total_pairs = block_len * cols
    weights = jnp.stack([coupling_a.reshape(-1), coupling_b.reshape(-1)])
    spans, width = piece_spans(depth)
    row_start = row_pos * row_len
    pieces = [
        jnp.pad(
            lax.dynamic_slice(densities, (row_start, lo), (row_len, hi - lo)),
            ((0, 0), (0, width - (hi - lo))),
        )
        for lo, hi in spans
    ]
    top_panel = jnp.where(panel_blocks[0] == top, 0, 1)
    other_panel = 1 - top_panel
    other = panel_blocks[other_panel]
    start_o = other * block_len + row_start
    start_top = top * block_len + row_start
    col_start = col_pos * block_len

    upper = col_pos >= half
    even_chip = (col_pos // 2) % 2 == 0
    sources = []
    for own_block, on_even in ((other, True), (top, False)):
        for parity in range(2):
            holds = col_pos % 2 == parity
            direct = even_chip if on_even else ~even_chip
            code = jnp.where(holds, jnp.where(direct, R1, R2), jnp.where(direct, R3, R4))
            code = jnp.where(upper, code, jnp.where(col_pos == own_block, OWN, 0))
            sources.append(code)
    late = jnp.where(upper | (col_pos <= other), 0, jnp.where(col_pos // 2 == other // 2, 1, 2 + col_pos % 2))
    flags = jnp.stack(
        sources
        + [late, col_pos >= other, col_pos >= top, other_panel, top_panel, start_o, start_top, col_start]
    ).astype(jnp.int32)

    def part(array, start, size):
        return lax.dynamic_slice_in_dim(array, start, size, 0)

    def picked(array):
        return jnp.concatenate(
            [part(array, col_start, block_len), part(array, start_o, row_len), part(array, start_top, row_len)]
        )

    anomal, direct = factors(picked(qp_index), amplitude_u, amplitude_v)
    label_all = picked(kpi_label)
    col_facts = jnp.stack(
        [
            anomal[:block_len],
            direct[:block_len],
            part(strength, col_start, block_len),
            label_all[:block_len].astype(jnp.float32),
        ]
    )
    row_facts = jnp.stack(
        [
            anomal[block_len:],
            direct[block_len:],
            picked(energies)[block_len:],
            picked(strength)[block_len:],
        ],
        axis=1,
    ).reshape(2, row_len, 4)
    row_labels = label_all[block_len:].reshape(2, row_len, 1)

    acc_shape = pltpu.VMEM((2, 2, row_len, block_len), jnp.float32)
    params = pltpu.CompilerParams(vmem_limit_bytes=VMEM_BYTES)

    def moved(o):
        got = []
        for i, piece in enumerate(pieces):
            q = i % 2
            if o != top:
                r1 = lax.ppermute(piece, "col", [(o, half + q), (top, half + 2 + q)])
            else:
                ra = lax.ppermute(piece, "col", [(top, half + 2 + q)])
                rb = lax.ppermute(piece, "col", [(top, half + q)])
                r1 = jnp.where(even_chip, rb, ra)
            r2 = lax.ppermute(r1, "col", [(half + q, half + 2 + q), (half + 2 + q, half + q)])
            core = [(half + q, half + 1 - q), (half + 2 + q, half + 3 - q)]
            r3 = lax.ppermute(r1, "col", core)
            r4 = lax.ppermute(r2, "col", core)
            if cols > 8:
                holds = col_pos % 2 == q
                now = [jnp.where(holds, r1, r3), jnp.where(holds, r2, r4)]
                for quad in range(1, cols // 8):
                    here = half + 4 * quad
                    pairs = [(here - 4 + j, here + j) for j in range(4)]
                    inside = (col_pos >= here) & (col_pos < here + 4)
                    now = [jnp.where(inside, lax.ppermute(x, "col", pairs), x) for x in now]
                r1, r2, r3, r4 = now + now
            got.append((r1, r2, r3, r4))
        return got

    def lower_half(o):
        own = lax.dynamic_slice_in_dim(densities, row_start, row_len, 0)
        l0 = l1 = l2 = own
        if o % 2 == 0:
            l0 = lax.ppermute(own, "col", [(o, o + 1)])
        chips = range(o // 2 + 1, half // 2)
        if chips:
            l1 = jnp.zeros_like(own)
            for m in chips:
                arrived = lax.ppermute(own, "col", [(o, 2 * m)])
                l1 = arrived if len(chips) == 1 else jnp.where(col_pos == 2 * m, arrived, l1)
            l2 = lax.ppermute(l1, "col", [(2 * m, 2 * m + 1) for m in chips])
        return l0, l1, l2

    def computed(got, lower):
        acc = None
        for i, (lo, hi) in enumerate(spans[:-1]):
            ins = [flags, pieces[i], *got[i], densities, weights]
            specs = [IN_SMEM] + [ANYWHERE] * 5 + [IN_VMEM] * 2
            if acc is not None:
                ins.append(acc)
                specs.append(IN_VMEM)
            acc = pl.pallas_call(
                functools.partial(piece_kernel, i % 2, lo, hi, acc is None),
                out_shape=acc_shape,
                in_specs=specs,
                out_specs=IN_VMEM,
                scratch_shapes=[
                    pltpu.VMEM((2, row_len, width), jnp.bfloat16),
                    pltpu.SemaphoreType.DMA((2,)),
                ],
                input_output_aliases={} if acc is None else {len(ins) - 1: 0},
                compiler_params=params,
                cost_estimate=cost(8 * row_len * block_len * (hi - lo), 4 * row_len * (hi - lo)),
                name="piece",
            )(*ins)
        if lower is not None:
            acc = pl.pallas_call(
                functools.partial(late_kernel, spans, width),
                out_shape=acc_shape,
                in_specs=[IN_SMEM] + [ANYWHERE] * 3 + [IN_VMEM] * 3,
                out_specs=IN_VMEM,
                scratch_shapes=[
                    pltpu.VMEM((row_len, depth), jnp.bfloat16),
                    pltpu.SemaphoreType.DMA,
                ],
                input_output_aliases={6: 0},
                compiler_params=params,
                cost_estimate=cost(1000000, 1000000),
                name="late",
            )(flags, *lower, densities, weights, acc)
        lo, hi = spans[-1]
        mat = jax.ShapeDtypeStruct((2, row_len, block_len), jnp.float32)
        mat_a, mat_b, resp, mirror = pl.pallas_call(
            functools.partial(last_kernel, (len(spans) - 1) % 2, lo, hi),
            out_shape=[
                mat,
                mat,
                jax.ShapeDtypeStruct((2, row_len), jnp.float32),
                jax.ShapeDtypeStruct((2, block_len), jnp.float32),
            ],
            in_specs=[IN_SMEM] + [ANYWHERE] * 5 + [IN_VMEM] * 6,
            out_specs=[ANYWHERE, ANYWHERE, IN_VMEM, IN_VMEM],
            scratch_shapes=[
                pltpu.VMEM((2, row_len, width), jnp.bfloat16),
                pltpu.VMEM((2, 2, row_len, block_len), jnp.float32),
                pltpu.SemaphoreType.DMA((2,)),
                pltpu.SemaphoreType.DMA((2, 2)),
            ],
            compiler_params=params,
            cost_estimate=cost(8 * row_len * block_len * (hi - lo), 16 * row_len * block_len),
            name="last",
        )(
            flags, pieces[-1], *got[-1], densities, weights,
            col_facts, row_facts, row_labels, acc,
        )
        response = all_sum(resp, "col") * (1.0 / math.sqrt(total_pairs))
        mirror = all_sum(mirror, "row") * (1.0 / math.sqrt(block_len))
        return mat_a, mat_b, response, mirror

    def branch(o):
        return computed(moved(o), lower_half(o) if o < top else None)

    def transfers(o):
        return moved(o), lower_half(o)

    if half <= BRANCHES:
        return lax.switch(other, [functools.partial(branch, o) for o in range(half)])
    return computed(*lax.switch(other, [functools.partial(transfers, o) for o in range(half)]))


def solution(mesh):
    placed = (P("col", None), P(), P(), P(), P(), P(), P(), P(), P(), P())
    return jax.shard_map(
        on_device,
        mesh=mesh,
        in_specs=placed,
        out_specs=(P(None, "row", "col"), P(None, "row", "col"), P(None, "row"), P(None, "col")),
        check_vma=False,
    )
```

```python
import functools
import math

import jax
import jax.numpy as jnp
from jax import lax
from jax.experimental import pallas as pl
from jax.experimental.pallas import tpu as pltpu
from jax.sharding import PartitionSpec as P

PAIRING = 1.0
HIGH = lax.Precision.HIGHEST
LANES = 128
PIECES = 3
PIECES_ONCE = 4
FIELDS = 8
BRANCHES = 4
IN_VMEM = pl.BlockSpec(memory_space=pltpu.VMEM)
IN_SMEM = pl.BlockSpec(memory_space=pltpu.SMEM)
ANYWHERE = pl.BlockSpec(memory_space=pl.ANY)

OWN, R1, R2, R3, R4 = 1, 2, 3, 4, 5
SRC_O, SRC_TOP, _, ACT_O, ACT_TOP, PANEL_O, PANEL_TOP, START_O, START_TOP, COL_POS, ROW_POS = (
    0, 2, 4, 5, 6, 7, 8, 9, 10, 11, 12,
)
BUSY, SEED = 13, 14
FIRST, SECOND, LABEL, STRENGTH, ENERGY = 0, 1, 2, 3, 4
ANOMAL, DIRECT = 0, 1


def up(size, step):
    return -(-size // step) * step


def vmem(value):
    return pltpu.with_memory_space_constraint(value, pltpu.VMEM)


def times(left, right):
    return lax.dot_general(
        left, right, (((1,), (1,)), ((), ())), preferred_element_type=jnp.float32
    )


def with_factors(facts, table):
    size = facts.shape[1]
    highs = table.shape[0] // 2
    low_ids = lax.broadcasted_iota(jnp.int32, (LANES, size), 0)
    high_ids = lax.broadcasted_iota(jnp.int32, (highs, size), 0)
    amps = []
    for field in (FIRST, SECOND):
        state = facts[field : field + 1].astype(jnp.int32)
        low = (low_ids == state % LANES).astype(jnp.float32)
        high = (high_ids == state // LANES).astype(jnp.float32)
        both = jnp.dot(table, low, precision=HIGH, preferred_element_type=jnp.float32)
        amps.append(jnp.sum(both[:highs] * high, axis=0, keepdims=True))
        amps.append(jnp.sum(both[highs:] * high, axis=0, keepdims=True))
    anomal = amps[0] * amps[3] + amps[1] * amps[2]
    direct = amps[0] * amps[2] - amps[1] * amps[3]
    return jnp.concatenate([anomal, direct, facts[2:]], axis=0)


def stretch(packed, start, size):
    window = up(size, LANES) + LANES
    base = pl.multiple_of(start // LANES * LANES, LANES)
    return pltpu.roll(packed[:, pl.ds(base, window)], window - start % LANES, 1)[:, :size]


def facts_kernel(flags, packed, table, dens, cols, rows):
    block_len, row_len = cols.shape[1], rows.shape[1]
    cols[...] = with_factors(stretch(packed, flags[COL_POS] * block_len, block_len), table[...])
    for slot in range(2):
        start = flags[START_O + slot] * block_len + flags[ROW_POS] * row_len
        facts = with_factors(stretch(packed, start, row_len), table[...])
        rows[slot] = jnp.concatenate([facts] * (LANES // FIELDS), axis=0).T


def cut_kernel(spans, flags, dens, *rest):
    pieces, buf, sem = rest[:-2], rest[-2], rest[-1]
    rows = buf.shape[0]
    copy = pltpu.make_async_copy(dens.at[pl.ds(flags[ROW_POS] * rows, rows)], buf, sem)
    copy.start()
    copy.wait()
    for (lo, hi), piece in zip(spans, pieces):
        width = piece.shape[1]
        if hi - lo < width:
            piece[...] = jnp.zeros_like(piece)
        piece[:, : hi - lo] = buf[:, lo:hi]


def pass_kernel(value, token, same):
    same[...] = value[...]


def seed_kernel(flags, value, instead, token, same):
    @pl.when(flags[SEED] > 0)
    def _():
        same[...] = instead[...]

    @pl.when(flags[SEED] == 0)
    def _():
        same[...] = value[...]


def row_tile(rows):
    return 48 if rows % 48 == 0 else rows


def weigh(x, at_lane, weights, start, width, lhs, base):
    rows = x.shape[0]
    tile = row_tile(rows)
    step_rows = up(rows, 16)

    def step(i, carry):
        at = 0 if tile == rows else pl.multiple_of(i * tile, 16)
        values = x[pl.ds(at, tile), pl.ds(at_lane, width)].astype(jnp.float32)
        for which in range(2):
            scale = weights[which : which + 1, pl.ds(start, width)]
            spot = pl.ds(base + which * step_rows + at, tile)
            lhs[spot, :width] = (values * scale).astype(jnp.bfloat16)
        return carry

    if tile == rows:
        step(0, 0)
    else:
        lax.fori_loop(0, rows // tile, step, 0)


def gather(entry, sources, flags, weights, span, lhs, base):
    for code, ref in sources:

        @pl.when(flags[entry] == code)
        def _():
            weigh(ref, 0, weights, span[0], span[1] - span[0], lhs, base)


def work(steps, flags, dens, weights, before, acc, lhs):
    block = acc.shape[0] // 2
    for pieces in steps:
        for n, (entry, span, sources) in enumerate(pieces):
            gather(entry, sources, flags, weights, span, lhs, n * block)
        if pieces[0][1] == pieces[1][1]:
            lo, hi = pieces[0][1]
            product = times(lhs[:, : hi - lo], dens[:, lo:hi])
            acc[...] = product if before is None else before[...] + product
        else:
            total = None
            for n, (_, (lo, hi), _) in enumerate(pieces):
                product = times(lhs[pl.ds(n * block, block), : hi - lo], dens[:, lo:hi])
                total = product if total is None else total + product
            acc[:block] = total if before is None else before[:block] + total
        before = acc


def spelled(plan, refs):
    return [
        [(entry, span, [(c, refs[r]) for c, r in found]) for entry, span, found in pieces]
        for pieces in plan
    ]


def first_kernel(plan, count, flags, *rest):
    dens, weights, _, acc, token, lhs = rest[count:]

    @pl.when(flags[BUSY] > 0)
    def _():
        work(spelled(plan, rest[:count]), flags, dens, weights, None, acc, lhs)

    token[...] = jnp.zeros_like(token)


def last_kernel(plan, twice, count, flags, *rest):
    refs = rest[:count]
    dens, weights, cols, rows, before = rest[count : count + 5]
    mat_a, mat_b, resp, mirror, acc, sums, lhs, made, out_sems = rest[count + 5 :]

    @pl.when(flags[BUSY] > 0)
    def _():
        work(spelled(plan, refs), flags, dens, weights, before, acc, lhs)

    block = acc.shape[0] // 2
    row_len, block_len = made.shape[2:]
    row_pad = block // 2
    tile = row_tile(row_len)
    resp[...] = jnp.zeros_like(resp)
    mirror[...] = jnp.zeros_like(mirror)

    def out_copies(slot, panel, at):
        return [
            pltpu.make_async_copy(made.at[slot, 0], mat_a.at[panel], out_sems.at[at, 0]),
            pltpu.make_async_copy(made.at[slot, 1], mat_b.at[panel], out_sems.at[at, 1]),
        ]

    def finish(slot, carry):
        panel = flags[PANEL_O + slot]

        @pl.when(flags[ACT_O + slot] > 0)
        def _():
            row_start = flags[START_O + slot] * block_len + flags[ROW_POS] * row_len
            shift = row_start - flags[COL_POS] * block_len

            def band(i, total):
                at = i * tile if tile == row_len else pl.multiple_of(i * tile, 16)
                span = pl.ds(at, tile)
                row = rows[slot, span, :]
                row_ids = lax.broadcasted_iota(jnp.int32, (tile, block_len), 0)
                col_ids = lax.broadcasted_iota(jnp.int32, (tile, block_len), 1)
                same = row[:, LABEL : LABEL + 1] == cols[LABEL : LABEL + 1]
                pair_a = row[:, ANOMAL : ANOMAL + 1] * cols[ANOMAL : ANOMAL + 1]
                pair_b = row[:, DIRECT : DIRECT + 1] * cols[DIRECT : DIRECT + 1]
                on_diagonal = row_ids + (at + shift) == col_ids
                full_a = acc[pl.ds(slot * block + at, tile), :] + jnp.where(same, PAIRING * pair_a, 0.0)
                full_a = full_a + jnp.where(on_diagonal, row[:, ENERGY : ENERGY + 1], 0.0)
                full_b = acc[pl.ds(slot * block + row_pad + at, tile), :]
                full_b = full_b + jnp.where(same, PAIRING * pair_b, 0.0)
                made[slot, 0, span, :] = full_a
                made[slot, 1, span, :] = full_b
                both = full_a + full_b
                across = jnp.sum(both * cols[STRENGTH : STRENGTH + 1], axis=1, keepdims=True)
                sums[span, :] = jnp.broadcast_to(across, (tile, LANES))
                return total + jnp.sum(both * row[:, STRENGTH : STRENGTH + 1], axis=0, keepdims=True)

            total = jnp.zeros((1, block_len), jnp.float32)
            if tile == row_len:
                total = band(0, total)
            else:
                total = lax.fori_loop(0, row_len // tile, band, total)
            mirror[pl.ds(panel, 1), :] = total
            resp[pl.ds(panel, 1), :] = sums[...].T[0:1]

        @pl.when(flags[ACT_O + slot] == 0)
        def _():
            made[slot] = jnp.zeros(made.shape[1:], made.dtype)

        for copy in out_copies(slot, panel, slot):
            copy.start()
        return carry

    if twice:
        finish(0, 0)
        for copy in out_copies(0, flags[PANEL_TOP], 1):
            copy.start()
        resp[pl.ds(flags[PANEL_TOP], 1), :] = resp[pl.ds(flags[PANEL_O], 1), :]
        mirror[pl.ds(flags[PANEL_TOP], 1), :] = mirror[pl.ds(flags[PANEL_O], 1), :]
    else:
        lax.fori_loop(0, 2, finish, 0)
    for slot in range(2):
        for copy in out_copies(0 if twice else slot, flags[PANEL_O + slot], slot):
            copy.wait()


def limit(mebibytes):
    return pltpu.CompilerParams(vmem_limit_bytes=mebibytes << 20)


def cost(flops, moved):
    return pl.CostEstimate(flops=flops, bytes_accessed=moved, transcendentals=0)


def all_sum(value, axis):
    size = lax.axis_size(axis)
    if size & (size - 1):
        return lax.psum(value, axis)
    step = 1
    while step < size:
        value = value + lax.ppermute(value, axis, [(i, i ^ step) for i in range(size)])
        step *= 2
    return value


def on_device(
    densities,
    coupling_a,
    coupling_b,
    energies,
    strength,
    qp_index,
    kpi_label,
    amplitude_u,
    amplitude_v,
    panel_blocks,
):
    block_len, depth = densities.shape
    row_count = lax.axis_size("row")
    cols = lax.axis_size("col")
    half = cols // 2
    top = half - 1
    row_len = block_len // row_count
    row_pad = up(row_len, 16)
    row_pos = lax.axis_index("row")
    col_pos = lax.axis_index("col")
    total_pairs = block_len * cols
    row_start = row_pos * row_len
    other = panel_blocks[0] + panel_blocks[1] - top
    top_panel = jnp.where(panel_blocks[0] == top, 0, 1)

    upper = col_pos >= half
    even_chip = (col_pos // 2) % 2 == 0

    def code(on_even, parity):
        direct = even_chip if on_even else ~even_chip
        holds = col_pos % 2 == parity
        return jnp.where(holds, jnp.where(direct, R1, R2), jnp.where(direct, R3, R4))

    def code_o(parity):
        same_quad = jnp.where(col_pos % 2 == parity, R2, R4)
        near = jnp.where(col_pos // 2 == other // 2, R3, same_quad)
        if cols > 8:
            near = jnp.int32(R1)
        low = jnp.where(col_pos == other, OWN, jnp.where(col_pos < other, 0, near))
        return jnp.where(upper, code(True, parity), low)

    def code_top(parity):
        return jnp.where(upper, code(False, parity), jnp.where(col_pos == top, OWN, 0))

    flags = jnp.stack(
        [
            code_o(0),
            code_o(1),
            code_top(0),
            code_top(1),
            jnp.int32(0),
            col_pos >= other,
            col_pos >= top,
            1 - top_panel,
            top_panel,
            other,
            jnp.int32(top),
            col_pos,
            row_pos,
            col_pos >= other,
            jnp.where(other == top, upper & ~even_chip, col_pos == other),
        ]
    ).astype(jnp.int32)

    def spans_of(count):
        width = up(-(-depth // count), LANES)
        return [(lo, min(depth, lo + width)) for lo in range(0, depth, width)]

    def cut(spans):
        width = spans[0][1]
        if row_len % 16 == 0:
            return pl.pallas_call(
                functools.partial(cut_kernel, spans),
                out_shape=[pltpu.VMEM((row_len, width), densities.dtype) for _ in spans],
                in_specs=[IN_SMEM, ANYWHERE],
                out_specs=[IN_VMEM for _ in spans],
                scratch_shapes=[
                    pltpu.VMEM((row_len, depth), densities.dtype),
                    pltpu.SemaphoreType.DMA,
                ],
                compiler_params=limit(6),
                name="cut",
            )(flags, densities)
        parts = [lax.dynamic_slice(densities, (row_start, lo), (row_len, hi - lo)) for lo, hi in spans]
        return [jnp.pad(x, ((0, 0), (0, width - x.shape[1]))) for x in parts]

    def seeded(o, came, own, token):
        value, instead = (came[0], own) if o != top else came
        if cols > 8:
            return jnp.where(flags[SEED] > 0, instead, value)
        return pl.pallas_call(
            seed_kernel,
            out_shape=pltpu.VMEM(value.shape, value.dtype),
            in_specs=[IN_SMEM] + [IN_VMEM] * 3,
            out_specs=IN_VMEM,
            input_output_aliases={1: 0},
            compiler_params=limit(4),
            name="seed",
        )(flags, vmem(value), vmem(instead), token)

    def to_chips(o, value, q):
        pairs = [(half + q, half + 2 + q), (half + 2 + q, half + q)]
        if o % 4 < 2 and o < top:
            pairs.append((o, o // 4 * 4 + 2 + q))
        return lax.ppermute(value, "col", pairs)

    def to_cores(o, value, q, with_o):
        pairs = [(half + q, half + 1 - q), (half + 2 + q, half + 3 - q)]
        if with_o and o % 2 == 0 and o < top:
            pairs.append((o, o + 1))
        if not with_o and o % 4 < 2 and o < top:
            pairs.append((o // 4 * 4 + 2 + q, o // 4 * 4 + 3 - q))
        return lax.ppermute(value, "col", pairs)

    def everywhere(o, value, r2, r3, r4, q):
        holds = col_pos % 2 == q
        now = [jnp.where(holds, value, r3), jnp.where(holds, r2, r4)]
        for quad in range(1, cols // 8):
            here = half + 4 * quad
            pairs = [(here - 4 + j, here + j) for j in range(4)]
            inside = (col_pos >= here) & (col_pos < here + 4)
            now = [jnp.where(inside, lax.ppermute(x, "col", pairs), x) for x in now]
        low = jnp.where(col_pos // 2 == o // 2, r3, now[1])
        later = range(o // 4 * 4 + 4, half, 4)
        for at in later:
            low = jnp.where(col_pos == at, lax.ppermute(value, "col", [(o, at)]), low)
        if later:
            beyond = col_pos >= later[0]
            got = lax.ppermute(low, "col", [(at, at + 1) for at in later])
            low = jnp.where(beyond & (col_pos % 4 == 1), got, low)
            pairs = [(at + j, at + j + 2) for at in later for j in range(2)]
            low = jnp.where(beyond & (col_pos % 4 >= 2), lax.ppermute(low, "col", pairs), low)
        first = jnp.where(upper, now[0], low)
        return [first, now[1], first, now[1]]

    def out_of_block(o, pieces, once):
        if o != top:
            return [
                [lax.ppermute(x, "col", [(o, half + i % 2), (top, half + 2 + i % 2)])]
                for i, x in reversed(list(enumerate(pieces)))
            ][::-1]
        pairs = list(zip(pieces[0::2], pieces[1::2])) if once else [(x, x) for x in pieces]
        got = []
        for i, (one, two) in enumerate(pairs):
            to_even = lax.ppermute(one, "col", [(top, half + i % 2)])
            to_odd = lax.ppermute(two, "col", [(top, half + 2 + i % 2)])
            got.append([to_even, to_odd])
        return got

    def after(value, token):
        return pl.pallas_call(
            pass_kernel,
            out_shape=pltpu.VMEM(value.shape, value.dtype),
            in_specs=[IN_VMEM] * 2,
            out_specs=IN_VMEM,
            input_output_aliases={0: 0},
            compiler_params=limit(4),
            name="after",
        )(vmem(value), token)

    def facts(dens):
        pairs = [qp_index[:, 0], qp_index[:, 1], kpi_label, strength, energies]
        pairs += [jnp.zeros_like(strength)] * (FIELDS - len(pairs))
        packed = jnp.stack([x.astype(jnp.float32) for x in pairs])
        packed = jnp.pad(packed, ((0, 0), (0, 2 * LANES)))
        table = jnp.concatenate([amplitude_u.reshape(-1, LANES), amplitude_v.reshape(-1, LANES)])
        return pl.pallas_call(
            facts_kernel,
            out_shape=[
                pltpu.VMEM((FIELDS, block_len), jnp.float32),
                pltpu.VMEM((2, row_len, LANES), jnp.float32),
            ],
            in_specs=[IN_SMEM] + [IN_VMEM] * 3,
            out_specs=[IN_VMEM] * 2,
            compiler_params=limit(4),
            name="facts",
        )(flags, packed, table, dens)

    def computed(o, spans, pieces, came, dens, col_facts, row_facts, twice):
        weights = vmem(jnp.stack([coupling_a.reshape(-1), coupling_b.reshape(-1)]))
        acc_shape = pltpu.VMEM((4 * row_pad, block_len), jnp.float32)
        lhs_shape = pltpu.VMEM((4 * row_pad, spans[0][1]), jnp.bfloat16)
        count = len(came)
        got = [list(arrays) for arrays in came]

        def plan_of(chunks):
            refs, plan = [], []
            for i in chunks:
                base = len(refs)
                refs += got[i]
                found = [(R1, base), (R2, base + 1), (R3, base + 2), (R4, base + 3)]
                own = [2 * i, 2 * i + 1] if twice else [i, i]
                step = []
                for which, p in zip((SRC_O, SRC_TOP), own):
                    step.append((which + i % 2, spans[p], [(OWN, len(refs))] + found))
                    refs.append(pieces[p])
                plan.append(step)
            return refs, plan

        refs, plan = plan_of(range(count - 1))
        ins = [flags, *[vmem(x) for x in refs], dens, weights, col_facts]
        products = sum(hi - lo for lo, hi in spans[: len(spans) - len(spans) // count])
        acc, token = pl.pallas_call(
            functools.partial(first_kernel, plan, len(refs)),
            out_shape=[acc_shape, pltpu.VMEM((8, LANES), jnp.float32)],
            in_specs=[IN_SMEM] + [IN_VMEM] * (len(ins) - 1),
            out_specs=[IN_VMEM] * 2,
            scratch_shapes=[lhs_shape],
            compiler_params=limit(14),
            cost_estimate=cost(8 * row_len * block_len * products, 4 * row_len * products),
            name="first",
        )(*ins)
        if len(got[-1]) < 4:
            got[-1][1] = after(got[-1][1], token)
            got[-1].append(to_cores(o, got[-1][1], (count - 1) % 2, False))
        refs, plan = plan_of([count - 1])
        mat = jax.ShapeDtypeStruct((2, row_len, block_len), jnp.float32)
        ins = [flags, *[vmem(x) for x in refs], dens, weights, col_facts, row_facts, acc]
        mat_a, mat_b, resp, mirror, _ = pl.pallas_call(
            functools.partial(last_kernel, plan, twice, len(refs)),
            out_shape=[
                mat,
                mat,
                jax.ShapeDtypeStruct((2, row_len), jnp.float32),
                jax.ShapeDtypeStruct((2, block_len), jnp.float32),
                acc_shape,
            ],
            in_specs=[IN_SMEM] + [IN_VMEM] * (len(ins) - 1),
            out_specs=[ANYWHERE, ANYWHERE] + [IN_VMEM] * 3,
            scratch_shapes=[
                pltpu.VMEM((row_len, LANES), jnp.float32),
                lhs_shape,
                pltpu.VMEM((2, 2, row_len, block_len), jnp.float32),
                pltpu.SemaphoreType.DMA((2, 2)),
            ],
            input_output_aliases={len(ins) - 1: 4},
            compiler_params=limit(14),
            cost_estimate=cost(8 * row_len * block_len * (depth - products), 16 * row_len * block_len),
            name="last",
        )(*ins)
        response = all_sum(resp, "col") * (1.0 / math.sqrt(total_pairs))
        mirror = all_sum(mirror, "row") * (1.0 / math.sqrt(block_len))
        return mat_a, mat_b, response, mirror

    def spread(o, i, came, own, token, to_the_end):
        q = i % 2
        value = seeded(o, came, own, token)
        r2 = to_chips(o, value, q)
        r3 = to_cores(o, value, q, True)
        if not to_the_end:
            return value, r2, r3
        return value, r2, r3, to_cores(o, r2, q, False)

    def branch(o):
        spans = spans_of(PIECES_ONCE if o == top else PIECES)
        pieces = cut(spans)
        came = out_of_block(o, pieces, True)
        dens = vmem(densities)
        col_facts, row_facts = facts(dens)
        last = len(came) - 1
        spreads = [spread(o, i, x, pieces[i], col_facts, i < last) for i, x in enumerate(came)]
        return computed(o, spans, pieces, spreads, dens, col_facts, row_facts, o == top)

    if half <= BRANCHES:
        return lax.switch(other, [functools.partial(branch, o) for o in range(half)])
    spans = spans_of(PIECES)
    pieces = cut(spans)

    def transfers(o):
        spreads = []
        for i, x in enumerate(out_of_block(o, pieces, False)):
            spreads.append(everywhere(o, *spread(o, i, x, pieces[i], None, True), i % 2))
        return spreads

    came = lax.switch(other, [functools.partial(transfers, o) for o in range(half)])
    dens = vmem(densities)
    return computed(None, spans, pieces, came, dens, *facts(dens), False)


def solution(mesh):
    placed = (P("col", None), P(), P(), P(), P(), P(), P(), P(), P(), P())
    return jax.shard_map(
        on_device,
        mesh=mesh,
        in_specs=placed,
        out_specs=(P(None, "row", "col"), P(None, "row", "col"), P(None, "row"), P(None, "col")),
        check_vma=False,
    )
```

```python
import functools
import math

import jax
import jax.numpy as jnp
from jax import lax
from jax.experimental import pallas as pl
from jax.experimental.pallas import tpu as pltpu
from jax.sharding import PartitionSpec as P

PAIRING = 1.0
HIGH = lax.Precision.HIGHEST
LANES = 128
PIECES = 2
PIECES_ONCE = 4
FIELDS = 8
FACT_TILE = 256
BRANCHES = 4
IN_VMEM = pl.BlockSpec(memory_space=pltpu.VMEM)
IN_SMEM = pl.BlockSpec(memory_space=pltpu.SMEM)
ANYWHERE = pl.BlockSpec(memory_space=pl.ANY)

OWN, R1, R2, R3, R4 = 1, 2, 3, 4, 5
SRC_O, SRC_TOP, _, ACT_O, ACT_TOP, PANEL_O, PANEL_TOP, START_O, START_TOP, COL_POS, ROW_POS = (
    0, 2, 4, 5, 6, 7, 8, 9, 10, 11, 12,
)
BUSY, SEED = 13, 14
FIRST, SECOND, LABEL, STRENGTH, ENERGY = 0, 1, 2, 3, 4
ANOMAL, DIRECT = 0, 1


def up(size, step):
    return -(-size // step) * step


def vmem(value):
    return pltpu.with_memory_space_constraint(value, pltpu.VMEM)


def times(left, right):
    return lax.dot_general(
        left, right, (((1,), (1,)), ((), ())), preferred_element_type=jnp.float32
    )


def with_factors(facts, table):
    size = facts.shape[1]
    highs = table.shape[0] // 2
    low_ids = lax.broadcasted_iota(jnp.int32, (LANES, size), 0)
    high_ids = lax.broadcasted_iota(jnp.int32, (highs, size), 0)
    amps = []
    for field in (FIRST, SECOND):
        state = facts[field : field + 1].astype(jnp.int32)
        low = (low_ids == state % LANES).astype(jnp.float32)
        high = (high_ids == state // LANES).astype(jnp.float32)
        both = jnp.dot(table, low, precision=HIGH, preferred_element_type=jnp.float32)
        amps.append(jnp.sum(both[:highs] * high, axis=0, keepdims=True))
        amps.append(jnp.sum(both[highs:] * high, axis=0, keepdims=True))
    anomal = amps[0] * amps[3] + amps[1] * amps[2]
    direct = amps[0] * amps[2] - amps[1] * amps[3]
    return jnp.concatenate([anomal, direct, facts[2:]], axis=0)


def stretch(packed, start, size):
    window = up(size, LANES) + LANES
    base = pl.multiple_of(start // LANES * LANES, LANES)
    return pltpu.roll(packed[:, pl.ds(base, window)], window - start % LANES, 1)[:, :size]


def facts_kernel(spans, flags, packed, table, dens, cols, rows, *rest):
    gathered = rest[-1] if not spans else rest[-3]
    if spans:
        cut_pieces(spans, flags, dens, rest[:-3], *rest[-2:])
    block_len, row_len = cols.shape[1], rows.shape[1]
    places = [(flags[COL_POS] * block_len, block_len)]
    for slot in range(2):
        start = flags[START_O + slot] * block_len + flags[ROW_POS] * row_len
        places.append((start, row_len))
    at = 0
    gathered[...] = jnp.zeros_like(gathered)
    spots = []
    for start, size in places:
        gathered[:, at : at + size] = stretch(packed, start, size)
        spots.append(at)
        at += up(size, FACT_TILE)

    def step(i, carry):
        span = pl.ds(pl.multiple_of(i * FACT_TILE, FACT_TILE), FACT_TILE)
        gathered[:, span] = with_factors(gathered[:, span], table[...])
        return carry

    lax.fori_loop(0, gathered.shape[1] // FACT_TILE, step, 0)
    cols[...] = gathered[:, :block_len]
    for slot in range(2):
        facts = gathered[:, spots[1 + slot] : spots[1 + slot] + row_len]
        rows[slot] = jnp.concatenate([facts] * (LANES // FIELDS), axis=0).T


def cut_pieces(spans, flags, dens, pieces, buf, sem):
    rows = buf.shape[0]
    lo, hi = spans[0][0], spans[-1][1]
    source = dens.at[pl.ds(flags[ROW_POS] * rows, rows), pl.ds(lo, hi - lo)]
    copy = pltpu.make_async_copy(source, buf, sem)
    copy.start()
    copy.wait()
    for (start, end), piece in zip(spans, pieces):
        width = piece.shape[1]

        def step(i, carry):
            span = pl.ds(pl.multiple_of(i * 16, 16), 16)
            if end - start < width:
                piece[span, :] = jnp.zeros((16, width), piece.dtype)
            piece[span, : end - start] = buf[span, start - lo : end - lo]
            return carry

        lax.fori_loop(0, rows // 16, step, 0)


def cut_kernel(spans, flags, dens, *rest):
    cut_pieces(spans, flags, dens, rest[:-2], *rest[-2:])


def by_bands(source, target):
    rows = source.shape[0]
    band = 16 if rows % 16 == 0 else rows

    def step(i, carry):
        span = pl.ds(pl.multiple_of(i * band, 16), band) if band < rows else slice(0, rows)
        target[span, :] = source[span, :]
        return carry

    lax.fori_loop(0, rows // band, step, 0)


def pass_kernel(value, token, same):
    by_bands(value, same)


def seed_kernel(flags, value, instead, token, same):
    @pl.when(flags[SEED] > 0)
    def _():
        by_bands(instead, same)

    @pl.when(flags[SEED] == 0)
    def _():
        by_bands(value, same)


def row_tile(rows):
    return 48 if rows % 48 == 0 else rows


def weigh(x, at_lane, weights, start, width, lhs, base):
    rows = x.shape[0]
    tile = row_tile(rows)
    step_rows = up(rows, 16)

    def step(i, carry):
        at = 0 if tile == rows else pl.multiple_of(i * tile, 16)
        values = x[pl.ds(at, tile), pl.ds(at_lane, width)].astype(jnp.float32)
        for which in range(2):
            scale = weights[which : which + 1, pl.ds(start, width)]
            spot = pl.ds(base + which * step_rows + at, tile)
            lhs[spot, :width] = (values * scale).astype(jnp.bfloat16)
        return carry

    if tile == rows:
        step(0, 0)
    else:
        lax.fori_loop(0, rows // tile, step, 0)


def gather(entry, sources, flags, weights, span, lhs, base):
    for code, ref in sources:

        @pl.when(flags[entry] == code)
        def _():
            weigh(ref, 0, weights, span[0], span[1] - span[0], lhs, base)


def work(steps, flags, dens, weights, before, acc, lhs, arrival=None):
    block = acc.shape[0] // 2
    width = lhs.shape[2]
    together = all(pieces[0][1] == pieces[1][1] for pieces in steps)
    rows = 2 * block if together else block
    parts = []
    for c, pieces in enumerate(steps):
        for n, (entry, span, sources) in enumerate(pieces):
            if together:
                gather(entry, sources, flags, weights, span, lhs.at[c], n * block)
            else:
                gather(entry, sources, flags, weights, span, lhs.at[2 * c + n], 0)
                parts.append(span)
        if together:
            parts.append(pieces[0][1])
    if before is None:
        sub = width // 2 if width % (2 * LANES) == 0 else width
        acc[...] = jnp.zeros_like(acc)
        arrival.wait()

        def step(i, carry):
            start = pl.multiple_of(parts[0][0] + i * sub, LANES)
            at = pl.multiple_of(i % (width // sub) * sub, LANES)
            acc[:rows] += times(
                lhs[i // (width // sub), :rows, pl.ds(at, sub)], dens[:, pl.ds(start, sub)]
            )
            return carry

        lax.fori_loop(0, len(parts) * (width // sub), step, 0)
        return
    total = before[:rows]
    for i, (lo, hi) in enumerate(parts):
        total = total + times(lhs[i, :rows, : hi - lo], dens[:, lo:hi])
    acc[:rows] = total


def spelled(plan, refs):
    return [
        [(entry, span, [(c, refs[r]) for c, r in found]) for entry, span, found in pieces]
        for pieces in plan
    ]


def first_kernel(plan, cut, count, flags, *rest):
    dens_from, weights, _, acc, token, dens, lhs, sems = rest[count:]
    ends = (pl.ds(0, cut), pl.ds(cut, dens.shape[1] - cut))
    copies = [
        pltpu.make_async_copy(dens_from.at[:, span], dens.at[:, span], sems.at[n])
        for n, span in enumerate(ends)
    ]

    @pl.when(flags[BUSY] > 0)
    def _():
        for copy in copies:
            copy.start()
        work(spelled(plan, rest[:count]), flags, dens, weights, None, acc, lhs, copies[0])
        copies[1].wait()

    token[...] = jnp.zeros_like(token)


def last_kernel(plan, twice, count, flags, *rest):
    refs = rest[:count]
    dens, weights, cols, rows, before = rest[count : count + 5]
    mat_a, mat_b, resp, mirror, acc, sums, lhs, made, out_sems = rest[count + 5 :]

    @pl.when(flags[BUSY] > 0)
    def _():
        work(spelled(plan, refs), flags, dens, weights, before, acc, lhs)

    block = acc.shape[0] // 2
    row_len, block_len = made.shape[2:]
    row_pad = block // 2
    tile = 48 if row_len % 48 == 0 else row_len
    resp[...] = jnp.zeros_like(resp)
    mirror[...] = jnp.zeros_like(mirror)

    def out_copies(slot, panel, at):
        return [
            pltpu.make_async_copy(made.at[slot, 0], mat_a.at[panel], out_sems.at[at, 0]),
            pltpu.make_async_copy(made.at[slot, 1], mat_b.at[panel], out_sems.at[at, 1]),
        ]

    def finish(slot, carry):
        panel = flags[PANEL_O + slot]

        @pl.when(flags[ACT_O + slot] > 0)
        def _():
            row_start = flags[START_O + slot] * block_len + flags[ROW_POS] * row_len
            shift = row_start - flags[COL_POS] * block_len

            def band(i, total):
                at = i * tile if tile == row_len else pl.multiple_of(i * tile, 16)
                span = pl.ds(at, tile)
                row = rows[slot, span, :]
                row_ids = lax.broadcasted_iota(jnp.int32, (tile, block_len), 0)
                col_ids = lax.broadcasted_iota(jnp.int32, (tile, block_len), 1)
                same = row[:, LABEL : LABEL + 1] == cols[LABEL : LABEL + 1]
                pair_a = row[:, ANOMAL : ANOMAL + 1] * cols[ANOMAL : ANOMAL + 1]
                pair_b = row[:, DIRECT : DIRECT + 1] * cols[DIRECT : DIRECT + 1]
                on_diagonal = row_ids + (at + shift) == col_ids
                full_a = acc[pl.ds(slot * block + at, tile), :] + jnp.where(same, PAIRING * pair_a, 0.0)
                full_a = full_a + jnp.where(on_diagonal, row[:, ENERGY : ENERGY + 1], 0.0)
                full_b = acc[pl.ds(slot * block + row_pad + at, tile), :]
                full_b = full_b + jnp.where(same, PAIRING * pair_b, 0.0)
                made[slot, 0, span, :] = full_a
                made[slot, 1, span, :] = full_b
                both = full_a + full_b
                across = jnp.sum(both * cols[STRENGTH : STRENGTH + 1], axis=1, keepdims=True)
                sums[span, :] = jnp.broadcast_to(across, (tile, LANES))
                return total + jnp.sum(both * row[:, STRENGTH : STRENGTH + 1], axis=0, keepdims=True)

            total = jnp.zeros((1, block_len), jnp.float32)
            if tile == row_len:
                total = band(0, total)
            else:
                total = lax.fori_loop(0, row_len // tile, band, total)
            mirror[pl.ds(panel, 1), :] = total
            resp[pl.ds(panel, 1), :] = sums[...].T[0:1]

        @pl.when(flags[ACT_O + slot] == 0)
        def _():
            made[slot] = jnp.zeros(made.shape[1:], made.dtype)

        for copy in out_copies(slot, panel, slot):
            copy.start()
        return carry

    if twice:
        finish(0, 0)
        for copy in out_copies(0, flags[PANEL_TOP], 1):
            copy.start()
        resp[pl.ds(flags[PANEL_TOP], 1), :] = resp[pl.ds(flags[PANEL_O], 1), :]
        mirror[pl.ds(flags[PANEL_TOP], 1), :] = mirror[pl.ds(flags[PANEL_O], 1), :]
    else:
        lax.fori_loop(0, 2, finish, 0)
    for slot in range(2):
        for copy in out_copies(0 if twice else slot, flags[PANEL_O + slot], slot):
            copy.wait()


def limit(mebibytes):
    return pltpu.CompilerParams(vmem_limit_bytes=mebibytes << 20)


def cost(flops, moved):
    return pl.CostEstimate(flops=flops, bytes_accessed=moved, transcendentals=0)


def all_sum(value, axis):
    size = lax.axis_size(axis)
    if size & (size - 1):
        return lax.psum(value, axis)
    step = 1
    while step < size:
        value = value + lax.ppermute(value, axis, [(i, i ^ step) for i in range(size)])
        step *= 2
    return value


def on_device(
    densities,
    coupling_a,
    coupling_b,
    energies,
    strength,
    qp_index,
    kpi_label,
    amplitude_u,
    amplitude_v,
    panel_blocks,
):
    block_len, depth = densities.shape
    row_count = lax.axis_size("row")
    cols = lax.axis_size("col")
    half = cols // 2
    top = half - 1
    row_len = block_len // row_count
    row_pad = up(row_len, 16)
    row_pos = lax.axis_index("row")
    col_pos = lax.axis_index("col")
    total_pairs = block_len * cols
    row_start = row_pos * row_len
    other = panel_blocks[0] + panel_blocks[1] - top
    top_panel = jnp.where(panel_blocks[0] == top, 0, 1)

    upper = col_pos >= half
    even_chip = (col_pos // 2) % 2 == 0

    def code(on_even, parity):
        direct = even_chip if on_even else ~even_chip
        holds = col_pos % 2 == parity
        return jnp.where(holds, jnp.where(direct, R1, R2), jnp.where(direct, R3, R4))

    def code_o(parity):
        same_quad = jnp.where(col_pos % 2 == parity, R2, R4)
        near = jnp.where(col_pos // 2 == other // 2, R3, same_quad)
        if cols > 8:
            near = jnp.int32(R1)
        low = jnp.where(col_pos == other, OWN, jnp.where(col_pos < other, 0, near))
        return jnp.where(upper, code(True, parity), low)

    def code_top(parity):
        return jnp.where(upper, code(False, parity), jnp.where(col_pos == top, OWN, 0))

    flags = jnp.stack(
        [
            code_o(0),
            code_o(1),
            code_top(0),
            code_top(1),
            jnp.int32(0),
            col_pos >= other,
            col_pos >= top,
            1 - top_panel,
            top_panel,
            other,
            jnp.int32(top),
            col_pos,
            row_pos,
            col_pos >= other,
            jnp.where(other == top, upper & ~even_chip, col_pos == other),
        ]
    ).astype(jnp.int32)

    in_kernels = row_len % 16 == 0

    def spans_of(count):
        width = up(-(-depth // count), LANES)
        return [(lo, min(depth, lo + width)) for lo in range(0, depth, width)]

    def cut(spans):
        width = spans[0][1]
        if in_kernels:
            ahead = spans[: len(spans) // 2]
            return pl.pallas_call(
                functools.partial(cut_kernel, ahead),
                out_shape=[pltpu.VMEM((row_len, width), densities.dtype) for _ in ahead],
                in_specs=[IN_SMEM, ANYWHERE],
                out_specs=[IN_VMEM for _ in ahead],
                scratch_shapes=cut_scratch(ahead),
                compiler_params=limit(6),
                name="cut",
            )(flags, densities)
        return sliced(spans)

    def sliced(spans):
        width = spans[0][1]
        parts = [lax.dynamic_slice(densities, (row_start, lo), (row_len, hi - lo)) for lo, hi in spans]
        return [jnp.pad(x, ((0, 0), (0, width - x.shape[1]))) for x in parts]

    def cut_scratch(spans):
        return [
            pltpu.VMEM((row_len, spans[-1][1] - spans[0][0]), densities.dtype),
            pltpu.SemaphoreType.DMA,
        ]

    def seeded(o, came, own, token):
        value, instead = (came[0], own) if o != top else came
        if cols > 8:
            return jnp.where(flags[SEED] > 0, instead, value)
        return pl.pallas_call(
            seed_kernel,
            out_shape=pltpu.VMEM(value.shape, value.dtype),
            in_specs=[IN_SMEM] + [IN_VMEM] * 3,
            out_specs=IN_VMEM,
            input_output_aliases={1: 0},
            compiler_params=limit(4),
            cost_estimate=cost(1, 1),
            name="seed",
        )(flags, vmem(value), vmem(instead), token)

    def to_chips(o, value, q):
        pairs = [(half + q, half + 2 + q), (half + 2 + q, half + q)]
        if o % 4 < 2 and o < top:
            pairs.append((o, o // 4 * 4 + 2 + q))
        return lax.ppermute(value, "col", pairs)

    def to_cores(o, value, q, with_o):
        pairs = [(half + q, half + 1 - q), (half + 2 + q, half + 3 - q)]
        if with_o and o % 2 == 0 and o < top:
            pairs.append((o, o + 1))
        if not with_o and o % 4 < 2 and o < top:
            pairs.append((o // 4 * 4 + 2 + q, o // 4 * 4 + 3 - q))
        return lax.ppermute(value, "col", pairs)

    def everywhere(o, value, r2, r3, r4, q):
        holds = col_pos % 2 == q
        now = [jnp.where(holds, value, r3), jnp.where(holds, r2, r4)]
        for quad in range(1, cols // 8):
            here = half + 4 * quad
            pairs = [(here - 4 + j, here + j) for j in range(4)]
            inside = (col_pos >= here) & (col_pos < here + 4)
            now = [jnp.where(inside, lax.ppermute(x, "col", pairs), x) for x in now]
        low = jnp.where(col_pos // 2 == o // 2, r3, now[1])
        later = range(o // 4 * 4 + 4, half, 4)
        for at in later:
            low = jnp.where(col_pos == at, lax.ppermute(value, "col", [(o, at)]), low)
        if later:
            beyond = col_pos >= later[0]
            got = lax.ppermute(low, "col", [(at, at + 1) for at in later])
            low = jnp.where(beyond & (col_pos % 4 == 1), got, low)
            pairs = [(at + j, at + j + 2) for at in later for j in range(2)]
            low = jnp.where(beyond & (col_pos % 4 >= 2), lax.ppermute(low, "col", pairs), low)
        first = jnp.where(upper, now[0], low)
        return [first, now[1], first, now[1]]

    def out_of_block(o, pieces, once):
        if o != top:
            return [
                [lax.ppermute(x, "col", [(o, half + i % 2), (top, half + 2 + i % 2)])]
                for i, x in enumerate(pieces)
            ]
        pairs = list(zip(pieces[0::2], pieces[1::2])) if once else [(x, x) for x in pieces]
        got = []
        for i, (one, two) in enumerate(pairs):
            to_even = lax.ppermute(one, "col", [(top, half + i % 2)])
            to_odd = lax.ppermute(two, "col", [(top, half + 2 + i % 2)])
            got.append([to_even, to_odd])
        return got

    def after(value, token):
        return pl.pallas_call(
            pass_kernel,
            out_shape=pltpu.VMEM(value.shape, value.dtype),
            in_specs=[IN_VMEM] * 2,
            out_specs=IN_VMEM,
            input_output_aliases={0: 0},
            compiler_params=limit(4),
            cost_estimate=cost(1, 1),
            name="after",
        )(vmem(value), token)

    def facts(spans, width):
        pairs = [qp_index[:, 0], qp_index[:, 1], kpi_label, strength, energies]
        pairs += [jnp.zeros_like(strength)] * (FIELDS - len(pairs))
        packed = jnp.stack([x.astype(jnp.float32) for x in pairs])
        packed = jnp.pad(packed, ((0, 0), (0, 2 * LANES)))
        table = jnp.concatenate([amplitude_u.reshape(-1, LANES), amplitude_v.reshape(-1, LANES)])
        gathered = pltpu.VMEM(
            (FIELDS, up(block_len, FACT_TILE) + 2 * up(row_len, FACT_TILE)), jnp.float32
        )
        return pl.pallas_call(
            functools.partial(facts_kernel, spans),
            out_shape=[
                pltpu.VMEM((FIELDS, block_len), jnp.float32),
                pltpu.VMEM((2, row_len, LANES), jnp.float32),
            ]
            + [pltpu.VMEM((row_len, width), densities.dtype) for _ in spans],
            in_specs=[IN_SMEM] + [IN_VMEM] * 2 + [ANYWHERE],
            out_specs=[IN_VMEM] * (2 + len(spans)),
            scratch_shapes=[gathered] + (cut_scratch(spans) if spans else []),
            compiler_params=limit(8),
            cost_estimate=cost(1, 1),
            name="facts",
        )(flags, packed, table, densities)

    def computed(o, spans, pieces, came, col_facts, row_facts, twice):
        weights = vmem(jnp.stack([coupling_a.reshape(-1), coupling_b.reshape(-1)]))
        acc_shape = pltpu.VMEM((4 * row_pad, block_len), jnp.float32)
        lhs_rows = 2 * row_pad if twice else 4 * row_pad
        lhs_shape = pltpu.VMEM((2 if twice else 1, lhs_rows, spans[0][1]), jnp.bfloat16)
        count = len(came)
        got = [list(arrays) for arrays in came]

        def plan_of(chunks):
            refs, plan = [], []
            for i in chunks:
                base = len(refs)
                refs += got[i]
                found = [(R1, base), (R2, base + 1), (R3, base + 2), (R4, base + 3)]
                own = [2 * i, 2 * i + 1] if twice else [i, i]
                step = []
                for which, p in zip((SRC_O, SRC_TOP), own):
                    step.append((which + i % 2, spans[p], [(OWN, len(refs))] + found))
                    refs.append(pieces[p])
                plan.append(step)
            return refs, plan

        refs, plan = plan_of(range(count - 1))
        ins = [flags, *[vmem(x) for x in refs], densities, weights, col_facts]
        ahead = spans[len(spans) - len(spans) // count][0]
        acc, token, dens = pl.pallas_call(
            functools.partial(first_kernel, plan, ahead, len(refs)),
            out_shape=[
                acc_shape,
                pltpu.VMEM((8, LANES), jnp.float32),
                pltpu.VMEM(densities.shape, densities.dtype),
            ],
            in_specs=[IN_SMEM] + [IN_VMEM] * len(refs) + [ANYWHERE] + [IN_VMEM] * 2,
            out_specs=[IN_VMEM] * 3,
            scratch_shapes=[lhs_shape, pltpu.SemaphoreType.DMA((2,))],
            compiler_params=limit(16),
            cost_estimate=cost(1, 1),
            name="first",
        )(*ins)
        if len(got[-1]) < 4:
            got[-1][1] = after(got[-1][1], token)
            got[-1].append(to_cores(o, got[-1][1], (count - 1) % 2, False))
        refs, plan = plan_of([count - 1])
        mat = jax.ShapeDtypeStruct((2, row_len, block_len), jnp.float32)
        ins = [flags, *[vmem(x) for x in refs], dens, weights, col_facts, row_facts, acc]
        mat_a, mat_b, resp, mirror, _ = pl.pallas_call(
            functools.partial(last_kernel, plan, twice, len(refs)),
            out_shape=[
                mat,
                mat,
                jax.ShapeDtypeStruct((2, row_len), jnp.float32),
                jax.ShapeDtypeStruct((2, block_len), jnp.float32),
                acc_shape,
            ],
            in_specs=[IN_SMEM] + [IN_VMEM] * (len(ins) - 1),
            out_specs=[ANYWHERE, ANYWHERE] + [IN_VMEM] * 3,
            scratch_shapes=[
                pltpu.VMEM((row_len, LANES), jnp.float32),
                lhs_shape,
                pltpu.VMEM((2, 2, row_len, block_len), jnp.float32),
                pltpu.SemaphoreType.DMA((2, 2)),
            ],
            input_output_aliases={len(ins) - 1: 4},
            compiler_params=limit(18),
            cost_estimate=cost(8 * row_len * block_len * spans[0][1], 16 * row_len * block_len),
            name="last",
        )(*ins)
        return mat_a, mat_b, resp, mirror

    def summed(mat_a, mat_b, resp, mirror):
        response = all_sum(resp, "col") * (1.0 / math.sqrt(total_pairs))
        mirror = all_sum(mirror, "row") * (1.0 / math.sqrt(block_len))
        return mat_a, mat_b, response, mirror

    def spread(o, i, value):
        q = i % 2
        return value, to_chips(o, value, q), to_cores(o, value, q, True)

    def branch(o):
        spans = spans_of(PIECES_ONCE if o == top else PIECES)
        width = spans[0][1]
        pieces = list(cut(spans))
        col_facts, row_facts, *others = facts(spans[len(pieces) :], width)
        pieces += others
        came = out_of_block(o, pieces, True)
        spreads = [
            list(spread(o, i, seeded(o, x, pieces[i], col_facts))) for i, x in enumerate(came)
        ]
        for i, now in enumerate(spreads[:-1]):
            now.append(to_cores(o, now[1], i % 2, False))
        return computed(o, spans, pieces, spreads, col_facts, row_facts, o == top)

    if half <= BRANCHES:
        return summed(*lax.switch(other, [functools.partial(branch, o) for o in range(half)]))
    spans = spans_of(PIECES)
    pieces = cut(spans) if not in_kernels else sliced(spans)

    def transfers(o):
        spreads = []
        for i, x in enumerate(out_of_block(o, pieces, False)):
            value = seeded(o, x, pieces[i], None)
            value, r2, r3 = spread(o, i, value)
            r4 = to_cores(o, r2, i % 2, False)
            spreads.append(everywhere(o, value, r2, r3, r4, i % 2))
        return spreads

    came = lax.switch(other, [functools.partial(transfers, o) for o in range(half)])
    col_facts, row_facts = facts([], 0)
    return summed(*computed(None, spans, pieces, came, col_facts, row_facts, False))


def solution(mesh):
    placed = (P("col", None), P(), P(), P(), P(), P(), P(), P(), P(), P())
    return jax.shard_map(
        on_device,
        mesh=mesh,
        in_specs=placed,
        out_specs=(P(None, "row", "col"), P(None, "row", "col"), P(None, "row"), P(None, "col")),
        check_vma=False,
    )
```

```python
import functools
import math

import jax
import jax.numpy as jnp
from jax import lax
from jax.experimental import pallas as pl
from jax.experimental.pallas import tpu as pltpu
from jax.sharding import PartitionSpec as P

PAIRING = 1.0
HIGH = lax.Precision.HIGHEST
LANES = 128
PIECES = 2
PIECES_ONCE = 4
FIELDS = 8
FACT_TILE = 256
BRANCHES = 4
IN_VMEM = pl.BlockSpec(memory_space=pltpu.VMEM)
IN_SMEM = pl.BlockSpec(memory_space=pltpu.SMEM)
ANYWHERE = pl.BlockSpec(memory_space=pl.ANY)

OWN, R1, R2, R3, R4 = 1, 2, 3, 4, 5
SRC_O, SRC_TOP, _, ACT_O, ACT_TOP, PANEL_O, PANEL_TOP, START_O, START_TOP, COL_POS, ROW_POS = (
    0, 2, 4, 5, 6, 7, 8, 9, 10, 11, 12,
)
BUSY, SEED = 13, 14
FIRST, SECOND, LABEL, STRENGTH, ENERGY = 0, 1, 2, 3, 4
ANOMAL, DIRECT = 0, 1


def up(size, step):
    return -(-size // step) * step


def vmem(value):
    return pltpu.with_memory_space_constraint(value, pltpu.VMEM)


def times(left, right):
    return lax.dot_general(
        left, right, (((1,), (1,)), ((), ())), preferred_element_type=jnp.float32
    )


def with_factors(facts, table):
    size = facts.shape[1]
    highs = table.shape[0] // 2
    low_ids = lax.broadcasted_iota(jnp.int32, (LANES, size), 0)
    high_ids = lax.broadcasted_iota(jnp.int32, (highs, size), 0)
    amps = []
    for field in (FIRST, SECOND):
        state = facts[field : field + 1].astype(jnp.int32)
        low = (low_ids == state % LANES).astype(jnp.float32)
        high = (high_ids == state // LANES).astype(jnp.float32)
        both = jnp.dot(table, low, precision=HIGH, preferred_element_type=jnp.float32)
        amps.append(jnp.sum(both[:highs] * high, axis=0, keepdims=True))
        amps.append(jnp.sum(both[highs:] * high, axis=0, keepdims=True))
    anomal = amps[0] * amps[3] + amps[1] * amps[2]
    direct = amps[0] * amps[2] - amps[1] * amps[3]
    return jnp.concatenate([anomal, direct, facts[2:]], axis=0)


def stretch(packed, start, size):
    window = up(size, LANES) + LANES
    base = pl.multiple_of(start // LANES * LANES, LANES)
    return pltpu.roll(packed[:, pl.ds(base, window)], window - start % LANES, 1)[:, :size]


def facts_kernel(spans, flags, packed, table, dens, cols, rows, *rest):
    gathered = rest[-1] if not spans else rest[-3]
    if spans:
        cut_pieces(spans, flags, dens, rest[:-3], *rest[-2:])
    block_len, row_len = cols.shape[1], rows.shape[1]
    places = [(flags[COL_POS] * block_len, block_len)]
    for slot in range(2):
        start = flags[START_O + slot] * block_len + flags[ROW_POS] * row_len
        places.append((start, row_len))
    at = 0
    gathered[...] = jnp.zeros_like(gathered)
    spots = []
    for start, size in places:
        gathered[:, at : at + size] = stretch(packed, start, size)
        spots.append(at)
        at += up(size, FACT_TILE)

    def step(i, carry):
        span = pl.ds(pl.multiple_of(i * FACT_TILE, FACT_TILE), FACT_TILE)
        gathered[:, span] = with_factors(gathered[:, span], table[...])
        return carry

    lax.fori_loop(0, gathered.shape[1] // FACT_TILE, step, 0)
    cols[...] = gathered[:, :block_len]
    for slot in range(2):
        facts = gathered[:, spots[1 + slot] : spots[1 + slot] + row_len]
        rows[slot] = jnp.concatenate([facts] * (LANES // FIELDS), axis=0).T


def cut_pieces(spans, flags, dens, pieces, buf, sem):
    rows = buf.shape[0]
    lo, hi = spans[0][0], spans[-1][1]
    source = dens.at[pl.ds(flags[ROW_POS] * rows, rows), pl.ds(lo, hi - lo)]
    copy = pltpu.make_async_copy(source, buf, sem)
    copy.start()
    copy.wait()
    for (start, end), piece in zip(spans, pieces):
        width = piece.shape[1]

        def step(i, carry):
            span = pl.ds(pl.multiple_of(i * 16, 16), 16)
            if end - start < width:
                piece[span, :] = jnp.zeros((16, width), piece.dtype)
            piece[span, : end - start] = buf[span, start - lo : end - lo]
            return carry

        lax.fori_loop(0, rows // 16, step, 0)


def cut_kernel(spans, flags, dens, *rest):
    cut_pieces(spans, flags, dens, rest[:-2], *rest[-2:])


def by_bands(source, target):
    rows = source.shape[0]
    band = 16 if rows % 16 == 0 else rows

    def step(i, carry):
        span = pl.ds(pl.multiple_of(i * band, 16), band) if band < rows else slice(0, rows)
        target[span, :] = source[span, :]
        return carry

    lax.fori_loop(0, rows // band, step, 0)


def pass_kernel(value, token, same):
    by_bands(value, same)


def seed_kernel(flags, value, instead, token, same):
    @pl.when(flags[SEED] > 0)
    def _():
        by_bands(instead, same)

    @pl.when(flags[SEED] == 0)
    def _():
        by_bands(value, same)


def row_tile(rows):
    return 48 if rows % 48 == 0 else rows


def weigh(x, at_lane, weights, start, width, lhs, base):
    rows = x.shape[0]
    tile = row_tile(rows)
    step_rows = up(rows, 16)

    def step(i, carry):
        at = 0 if tile == rows else pl.multiple_of(i * tile, 16)
        values = x[pl.ds(at, tile), pl.ds(at_lane, width)].astype(jnp.float32)
        for which in range(2):
            scale = weights[which : which + 1, pl.ds(start, width)]
            spot = pl.ds(base + which * step_rows + at, tile)
            lhs[spot, :width] = (values * scale).astype(jnp.bfloat16)
        return carry

    if tile == rows:
        step(0, 0)
    else:
        lax.fori_loop(0, rows // tile, step, 0)


def gather(entry, sources, flags, weights, span, lhs, base):
    for code, ref in sources:

        @pl.when(flags[entry] == code)
        def _():
            weigh(ref, 0, weights, span[0], span[1] - span[0], lhs, base)


def work(steps, flags, dens, weights, before, acc, lhs, arrival=None):
    block = acc.shape[0] // 2
    width = lhs.shape[2]
    together = all(pieces[0][1] == pieces[1][1] for pieces in steps)
    rows = 2 * block if together else block
    parts = []
    for c, pieces in enumerate(steps):
        for n, (entry, span, sources) in enumerate(pieces):
            if together:
                gather(entry, sources, flags, weights, span, lhs.at[c], n * block)
            else:
                gather(entry, sources, flags, weights, span, lhs.at[2 * c + n], 0)
                parts.append(span)
        if together:
            parts.append(pieces[0][1])
    if before is None:
        sub = width // 2 if width % (2 * LANES) == 0 else width
        acc[...] = jnp.zeros_like(acc)
        arrival.wait()

        def step(i, carry):
            start = pl.multiple_of(parts[0][0] + i * sub, LANES)
            at = pl.multiple_of(i % (width // sub) * sub, LANES)
            acc[:rows] += times(
                lhs[i // (width // sub), :rows, pl.ds(at, sub)], dens[:, pl.ds(start, sub)]
            )
            return carry

        lax.fori_loop(0, len(parts) * (width // sub), step, 0)
        return
    total = before[:rows]
    for i, (lo, hi) in enumerate(parts):
        total = total + times(lhs[i, :rows, : hi - lo], dens[:, lo:hi])
    acc[:rows] = total


def spelled(plan, refs):
    return [
        [(entry, span, [(c, refs[r]) for c, r in found]) for entry, span, found in pieces]
        for pieces in plan
    ]


def first_kernel(plan, cut, count, flags, *rest):
    dens_from, weights, _, acc, token, dens, lhs, sems = rest[count:]
    ends = (pl.ds(0, cut), pl.ds(cut, dens.shape[1] - cut))
    copies = [
        pltpu.make_async_copy(dens_from.at[:, span], dens.at[:, span], sems.at[n])
        for n, span in enumerate(ends)
    ]

    @pl.when(flags[BUSY] > 0)
    def _():
        for copy in copies:
            copy.start()
        work(spelled(plan, rest[:count]), flags, dens, weights, None, acc, lhs, copies[0])
        copies[1].wait()

    token[...] = jnp.zeros_like(token)


def last_kernel(plan, twice, count, flags, *rest):
    refs = rest[:count]
    dens, weights, cols, rows, before = rest[count : count + 5]
    mat_a, mat_b, resp, mirror, acc, sums, lhs, made, out_sems = rest[count + 5 :]

    @pl.when(flags[BUSY] > 0)
    def _():
        work(spelled(plan, refs), flags, dens, weights, before, acc, lhs)

    block = acc.shape[0] // 2
    row_len, block_len = made.shape[2:]
    row_pad = block // 2
    tile = 48 if row_len % 48 == 0 else row_len
    resp[...] = jnp.zeros_like(resp)
    mirror[...] = jnp.zeros_like(mirror)

    def out_copies(slot, panel, at):
        return [
            pltpu.make_async_copy(made.at[slot, 0], mat_a.at[panel], out_sems.at[at, 0]),
            pltpu.make_async_copy(made.at[slot, 1], mat_b.at[panel], out_sems.at[at, 1]),
        ]

    def finish(slot, carry):
        panel = flags[PANEL_O + slot]

        @pl.when(flags[ACT_O + slot] > 0)
        def _():
            row_start = flags[START_O + slot] * block_len + flags[ROW_POS] * row_len
            shift = row_start - flags[COL_POS] * block_len

            def band(i, total):
                at = i * tile if tile == row_len else pl.multiple_of(i * tile, 16)
                span = pl.ds(at, tile)
                row = rows[slot, span, :]
                row_ids = lax.broadcasted_iota(jnp.int32, (tile, block_len), 0)
                col_ids = lax.broadcasted_iota(jnp.int32, (tile, block_len), 1)
                same = row[:, LABEL : LABEL + 1] == cols[LABEL : LABEL + 1]
                pair_a = row[:, ANOMAL : ANOMAL + 1] * cols[ANOMAL : ANOMAL + 1]
                pair_b = row[:, DIRECT : DIRECT + 1] * cols[DIRECT : DIRECT + 1]
                on_diagonal = row_ids + (at + shift) == col_ids
                full_a = acc[pl.ds(slot * block + at, tile), :] + jnp.where(same, PAIRING * pair_a, 0.0)
                full_a = full_a + jnp.where(on_diagonal, row[:, ENERGY : ENERGY + 1], 0.0)
                full_b = acc[pl.ds(slot * block + row_pad + at, tile), :]
                full_b = full_b + jnp.where(same, PAIRING * pair_b, 0.0)
                made[slot, 0, span, :] = full_a
                made[slot, 1, span, :] = full_b
                both = full_a + full_b
                across = jnp.sum(both * cols[STRENGTH : STRENGTH + 1], axis=1, keepdims=True)
                sums[span, :] = jnp.broadcast_to(across, (tile, LANES))
                return total + jnp.sum(both * row[:, STRENGTH : STRENGTH + 1], axis=0, keepdims=True)

            total = jnp.zeros((1, block_len), jnp.float32)
            if tile == row_len:
                total = band(0, total)
            else:
                total = lax.fori_loop(0, row_len // tile, band, total)
            mirror[pl.ds(panel, 1), :] = total
            resp[pl.ds(panel, 1), :] = sums[...].T[0:1]

        @pl.when(flags[ACT_O + slot] == 0)
        def _():
            made[slot] = jnp.zeros(made.shape[1:], made.dtype)

        for copy in out_copies(slot, panel, slot):
            copy.start()
        return carry

    if twice:
        finish(0, 0)
        for copy in out_copies(0, flags[PANEL_TOP], 1):
            copy.start()
        resp[pl.ds(flags[PANEL_TOP], 1), :] = resp[pl.ds(flags[PANEL_O], 1), :]
        mirror[pl.ds(flags[PANEL_TOP], 1), :] = mirror[pl.ds(flags[PANEL_O], 1), :]
    else:
        lax.fori_loop(0, 2, finish, 0)
    for slot in range(2):
        for copy in out_copies(0 if twice else slot, flags[PANEL_O + slot], slot):
            copy.wait()


def limit(mebibytes):
    return pltpu.CompilerParams(vmem_limit_bytes=mebibytes << 20)


def cost(flops, moved):
    return pl.CostEstimate(flops=flops, bytes_accessed=moved, transcendentals=0)


def both_sums(one, one_axis, two, two_axis):
    sizes = [lax.axis_size(one_axis), lax.axis_size(two_axis)]
    if any(size & (size - 1) for size in sizes):
        return lax.psum(one, one_axis), lax.psum(two, two_axis)
    length = one.shape[1]
    room = up(length, LANES)
    now = jnp.concatenate([jnp.pad(one, ((0, 0), (0, room - length))), two], axis=1)
    step = 1
    while step < max(sizes):
        parts = []
        for part, axis, size in ((now[:, :room], one_axis, sizes[0]), (now[:, room:], two_axis, sizes[1])):
            if step < size:
                part = part + lax.ppermute(part, axis, [(i, i ^ step) for i in range(size)])
            parts.append(part)
        now = jnp.concatenate(parts, axis=1)
        step *= 2
    return now[:, :length], now[:, room:]


def on_device(
    densities,
    coupling_a,
    coupling_b,
    energies,
    strength,
    qp_index,
    kpi_label,
    amplitude_u,
    amplitude_v,
    panel_blocks,
):
    block_len, depth = densities.shape
    row_count = lax.axis_size("row")
    cols = lax.axis_size("col")
    half = cols // 2
    top = half - 1
    row_len = block_len // row_count
    row_pad = up(row_len, 16)
    row_pos = lax.axis_index("row")
    col_pos = lax.axis_index("col")
    total_pairs = block_len * cols
    row_start = row_pos * row_len
    other = panel_blocks[0] + panel_blocks[1] - top
    top_panel = jnp.where(panel_blocks[0] == top, 0, 1)

    upper = col_pos >= half
    even_chip = (col_pos // 2) % 2 == 0

    def code(on_even, parity):
        direct = even_chip if on_even else ~even_chip
        holds = col_pos % 2 == parity
        return jnp.where(holds, jnp.where(direct, R1, R2), jnp.where(direct, R3, R4))

    def code_o(parity):
        same_quad = jnp.where(col_pos % 2 == parity, R2, R4)
        near = jnp.where(col_pos // 2 == other // 2, R3, same_quad)
        if cols > 8:
            near = jnp.int32(R1)
        low = jnp.where(col_pos == other, OWN, jnp.where(col_pos < other, 0, near))
        return jnp.where(upper, code(True, parity), low)

    def code_top(parity):
        return jnp.where(upper, code(False, parity), jnp.where(col_pos == top, OWN, 0))

    flags = jnp.stack(
        [
            code_o(0),
            code_o(1),
            code_top(0),
            code_top(1),
            jnp.int32(0),
            col_pos >= other,
            col_pos >= top,
            1 - top_panel,
            top_panel,
            other,
            jnp.int32(top),
            col_pos,
            row_pos,
            col_pos >= other,
            jnp.where(other == top, upper & ~even_chip, col_pos == other),
        ]
    ).astype(jnp.int32)

    in_kernels = row_len % 16 == 0

    def spans_of(count):
        width = up(-(-depth // count), LANES)
        return [(lo, min(depth, lo + width)) for lo in range(0, depth, width)]

    def cut(spans):
        width = spans[0][1]
        if in_kernels:
            ahead = spans[: len(spans) // 2]
            return pl.pallas_call(
                functools.partial(cut_kernel, ahead),
                out_shape=[pltpu.VMEM((row_len, width), densities.dtype) for _ in ahead],
                in_specs=[IN_SMEM, ANYWHERE],
                out_specs=[IN_VMEM for _ in ahead],
                scratch_shapes=cut_scratch(ahead),
                compiler_params=limit(6),
                name="cut",
            )(flags, densities)
        return sliced(spans)

    def sliced(spans):
        width = spans[0][1]
        parts = [lax.dynamic_slice(densities, (row_start, lo), (row_len, hi - lo)) for lo, hi in spans]
        return [jnp.pad(x, ((0, 0), (0, width - x.shape[1]))) for x in parts]

    def cut_scratch(spans):
        return [
            pltpu.VMEM((row_len, spans[-1][1] - spans[0][0]), densities.dtype),
            pltpu.SemaphoreType.DMA,
        ]

    def seeded(o, came, own, token):
        value, instead = (came[0], own) if o != top else came
        if cols > 8:
            return jnp.where(flags[SEED] > 0, instead, value)
        return pl.pallas_call(
            seed_kernel,
            out_shape=pltpu.VMEM(value.shape, value.dtype),
            in_specs=[IN_SMEM] + [IN_VMEM] * 3,
            out_specs=IN_VMEM,
            input_output_aliases={1: 0},
            compiler_params=limit(4),
            cost_estimate=cost(1, 1),
            name="seed",
        )(flags, vmem(value), vmem(instead), token)

    def to_chips(o, value, q):
        pairs = [(half + q, half + 2 + q), (half + 2 + q, half + q)]
        if o % 4 < 2 and o < top:
            pairs.append((o, o // 4 * 4 + 2 + q))
        return lax.ppermute(value, "col", pairs)

    def to_cores(value):
        return lax.ppermute(value, "col", [(i, i ^ 1) for i in range(cols)])

    def everywhere(o, value, r2, r3, r4, q):
        holds = col_pos % 2 == q
        now = [jnp.where(holds, value, r3), jnp.where(holds, r2, r4)]
        for quad in range(1, cols // 8):
            here = half + 4 * quad
            pairs = [(here - 4 + j, here + j) for j in range(4)]
            inside = (col_pos >= here) & (col_pos < here + 4)
            now = [jnp.where(inside, lax.ppermute(x, "col", pairs), x) for x in now]
        low = jnp.where(col_pos // 2 == o // 2, r3, now[1])
        later = range(o // 4 * 4 + 4, half, 4)
        for at in later:
            low = jnp.where(col_pos == at, lax.ppermute(value, "col", [(o, at)]), low)
        if later:
            beyond = col_pos >= later[0]
            got = lax.ppermute(low, "col", [(at, at + 1) for at in later])
            low = jnp.where(beyond & (col_pos % 4 == 1), got, low)
            pairs = [(at + j, at + j + 2) for at in later for j in range(2)]
            low = jnp.where(beyond & (col_pos % 4 >= 2), lax.ppermute(low, "col", pairs), low)
        first = jnp.where(upper, now[0], low)
        return [first, now[1], first, now[1]]

    def out_of_block(o, pieces, once):
        if o != top:
            return [
                [lax.ppermute(x, "col", [(o, half + i % 2), (top, half + 2 + i % 2)])]
                for i, x in enumerate(pieces)
            ]
        pairs = list(zip(pieces[0::2], pieces[1::2])) if once else [(x, x) for x in pieces]
        got = []
        for i, (one, two) in enumerate(pairs):
            to_even = lax.ppermute(one, "col", [(top, half + i % 2)])
            to_odd = lax.ppermute(two, "col", [(top, half + 2 + i % 2)])
            got.append([to_even, to_odd])
        return got

    def after(value, token):
        return pl.pallas_call(
            pass_kernel,
            out_shape=pltpu.VMEM(value.shape, value.dtype),
            in_specs=[IN_VMEM] * 2,
            out_specs=IN_VMEM,
            input_output_aliases={0: 0},
            compiler_params=limit(4),
            cost_estimate=cost(1, 1),
            name="after",
        )(vmem(value), token)

    def facts(spans, width):
        pairs = [qp_index[:, 0], qp_index[:, 1], kpi_label, strength, energies]
        pairs += [jnp.zeros_like(strength)] * (FIELDS - len(pairs))
        packed = jnp.stack([x.astype(jnp.float32) for x in pairs])
        packed = jnp.pad(packed, ((0, 0), (0, 2 * LANES)))
        table = jnp.concatenate([amplitude_u.reshape(-1, LANES), amplitude_v.reshape(-1, LANES)])
        gathered = pltpu.VMEM(
            (FIELDS, up(block_len, FACT_TILE) + 2 * up(row_len, FACT_TILE)), jnp.float32
        )
        return pl.pallas_call(
            functools.partial(facts_kernel, spans),
            out_shape=[
                pltpu.VMEM((FIELDS, block_len), jnp.float32),
                pltpu.VMEM((2, row_len, LANES), jnp.float32),
            ]
            + [pltpu.VMEM((row_len, width), densities.dtype) for _ in spans],
            in_specs=[IN_SMEM] + [IN_VMEM] * 2 + [ANYWHERE],
            out_specs=[IN_VMEM] * (2 + len(spans)),
            scratch_shapes=[gathered] + (cut_scratch(spans) if spans else []),
            compiler_params=limit(8),
            cost_estimate=cost(1, 1),
            name="facts",
        )(flags, packed, table, densities)

    def computed(o, spans, pieces, came, col_facts, row_facts, twice):
        weights = vmem(jnp.stack([coupling_a.reshape(-1), coupling_b.reshape(-1)]))
        acc_shape = pltpu.VMEM((4 * row_pad, block_len), jnp.float32)
        lhs_rows = 2 * row_pad if twice else 4 * row_pad
        lhs_shape = pltpu.VMEM((2 if twice else 1, lhs_rows, spans[0][1]), jnp.bfloat16)
        count = len(came)
        got = [list(arrays) for arrays in came]

        def plan_of(chunks):
            refs, plan = [], []
            for i in chunks:
                base = len(refs)
                refs += got[i]
                found = [(R1, base), (R2, base + 1), (R3, base + 2), (R4, base + 3)]
                own = [2 * i, 2 * i + 1] if twice else [i, i]
                step = []
                for which, p in zip((SRC_O, SRC_TOP), own):
                    step.append((which + i % 2, spans[p], [(OWN, len(refs))] + found))
                    refs.append(pieces[p])
                plan.append(step)
            return refs, plan

        refs, plan = plan_of(range(count - 1))
        ins = [flags, *[vmem(x) for x in refs], densities, weights, col_facts]
        ahead = spans[len(spans) - len(spans) // count][0]
        acc, token, dens = pl.pallas_call(
            functools.partial(first_kernel, plan, ahead, len(refs)),
            out_shape=[
                acc_shape,
                pltpu.VMEM((8, LANES), jnp.float32),
                pltpu.VMEM(densities.shape, densities.dtype),
            ],
            in_specs=[IN_SMEM] + [IN_VMEM] * len(refs) + [ANYWHERE] + [IN_VMEM] * 2,
            out_specs=[IN_VMEM] * 3,
            scratch_shapes=[lhs_shape, pltpu.SemaphoreType.DMA((2,))],
            compiler_params=limit(16),
            cost_estimate=cost(1, 1),
            name="first",
        )(*ins)
        if len(got[-1]) < 4:
            got[-1][1] = after(got[-1][1], token)
            got[-1].append(to_cores(got[-1][1]))
        refs, plan = plan_of([count - 1])
        mat = jax.ShapeDtypeStruct((2, row_len, block_len), jnp.float32)
        ins = [flags, *[vmem(x) for x in refs], dens, weights, col_facts, row_facts, acc]
        mat_a, mat_b, resp, mirror, _ = pl.pallas_call(
            functools.partial(last_kernel, plan, twice, len(refs)),
            out_shape=[
                mat,
                mat,
                jax.ShapeDtypeStruct((2, row_len), jnp.float32),
                jax.ShapeDtypeStruct((2, block_len), jnp.float32),
                acc_shape,
            ],
            in_specs=[IN_SMEM] + [IN_VMEM] * (len(ins) - 1),
            out_specs=[ANYWHERE, ANYWHERE] + [IN_VMEM] * 3,
            scratch_shapes=[
                pltpu.VMEM((row_len, LANES), jnp.float32),
                lhs_shape,
                pltpu.VMEM((2, 2, row_len, block_len), jnp.float32),
                pltpu.SemaphoreType.DMA((2, 2)),
            ],
            input_output_aliases={len(ins) - 1: 4},
            compiler_params=limit(18),
            cost_estimate=cost(8 * row_len * block_len * spans[0][1], 16 * row_len * block_len),
            name="last",
        )(*ins)
        return mat_a, mat_b, resp, mirror

    def summed(mat_a, mat_b, resp, mirror):
        response, mirror = both_sums(resp, "col", mirror, "row")
        response = response * (1.0 / math.sqrt(total_pairs))
        return mat_a, mat_b, response, mirror * (1.0 / math.sqrt(block_len))

    def spread(o, i, value):
        q = i % 2
        return value, to_chips(o, value, q), to_cores(value)

    def branch(o):
        spans = spans_of(PIECES_ONCE if o == top else PIECES)
        width = spans[0][1]
        pieces = list(cut(spans))
        col_facts, row_facts, *others = facts(spans[len(pieces) :], width)
        pieces += others
        came = out_of_block(o, pieces, True)
        spreads = [
            list(spread(o, i, seeded(o, x, pieces[i], col_facts))) for i, x in enumerate(came)
        ]
        for i, now in enumerate(spreads[:-1]):
            now.append(to_cores(now[1]))
        return computed(o, spans, pieces, spreads, col_facts, row_facts, o == top)

    if half <= BRANCHES:
        return summed(*lax.switch(other, [functools.partial(branch, o) for o in range(half)]))
    spans = spans_of(PIECES)
    pieces = cut(spans) if not in_kernels else sliced(spans)

    def transfers(o):
        spreads = []
        for i, x in enumerate(out_of_block(o, pieces, False)):
            value = seeded(o, x, pieces[i], None)
            value, r2, r3 = spread(o, i, value)
            r4 = to_cores(r2)
            spreads.append(everywhere(o, value, r2, r3, r4, i % 2))
        return spreads

    came = lax.switch(other, [functools.partial(transfers, o) for o in range(half)])
    col_facts, row_facts = facts([], 0)
    return summed(*computed(None, spans, pieces, came, col_facts, row_facts, False))


def solution(mesh):
    placed = (P("col", None), P(), P(), P(), P(), P(), P(), P(), P(), P())
    return jax.shard_map(
        on_device,
        mesh=mesh,
        in_specs=placed,
        out_specs=(P(None, "row", "col"), P(None, "row", "col"), P(None, "row"), P(None, "col")),
        check_vma=False,
    )
```
